256 devices in a mesh: dp: 32 (over y, z), tensor: 8 (over x, core).
Axes of the slice: x: 4, y: 4, z: 8, core: 2. Of those that a mesh axis runs over, the one named last changes fastest.
Arguments:
- tokens: bfloat16 [12288, 16384], P('dp', 'tensor'), may hold values from -6 to 6
- gate_weight: bfloat16 [16384, 1024], P(None, 'tensor'), may hold values from -0.046875 to 0.046875
- up_weight: bfloat16 [16384, 1024], P(None, 'tensor'), may hold values from -0.046875 to 0.046875
- hidden_grad: bfloat16 [12288, 1024], P('dp', 'tensor'), may hold values from -6 to 6
- mb_lengths: int32 [32, 4], P('dp'), may hold values from 48 to 96, as said below
Outputs:
- gate_grad: float32 [16384, 1024], P('dp', 'tensor')
- up_grad: float32 [16384, 1024], P('dp', 'tensor')
The draws below stay inside these ranges and needn't reach their ends.
Inputs may be any that keep to these rules, and one draw needn't show every extreme that they name: `mb_lengths`: every dp index holds 4 microbatches of 48 to 96 tokens each; in every draw the microbatches of one dp index all have the largest length, so that all its slots are held.
All inputs are finite; a program needn't handle non-finite values.
Results may differ from the reference program's by a relative error of at most 0.0029.
Values may be sent and summed in bfloat16 or wider, within the bound.
No kernel may reach another device: no remote copies, remote signals or barrier semaphores. Data moves between devices by JAX's collectives and lax.ppermute only.
A program may use at most 128 MiB of HBM per device.

```python
import jax
import jax.numpy as jnp

D = 16384
SLAB = 1024
MB_DEV = 4
TOK_DEV = 384
TOKENS = 12288
N_DP = 32


def draw_mb_lengths(key, part):
    key = jax.random.fold_in(key, 11)
    first_key, second_key = jax.random.split(key)
    longest = TOK_DEV // MB_DEV
    shortest = longest // 2
    drawn = jax.random.randint(first_key, (N_DP, MB_DEV), shortest, longest + 1)
    filled = jax.random.randint(second_key, (), 0, N_DP)
    ranks = jnp.arange(N_DP, dtype=jnp.int32)[:, None]
    return jnp.where(ranks == filled, longest, drawn).astype(jnp.int32)


def steps_of(own_key, extent, pieces, smallest, largest):
    def one(axis_at, shards_of):
        draws = jax.random.uniform(jax.random.fold_in(jax.random.fold_in(own_key, 6), axis_at), (shards_of,), jnp.float32, smallest / len(pieces), largest / len(pieces))
        return jnp.repeat(jnp.exp(draws), extent[axis_at] // shards_of).reshape((-1,) + (1,) * (len(extent) - axis_at - 1))

    factor_of = one(*pieces[0])
    for cut in pieces[1:]:
        factor_of = factor_of * one(*cut)
    return factor_of


def gaussian(own_key, dims, width, most, pieces=(), kind=jnp.bfloat16):
    loudness = steps_of(own_key, dims, pieces, -0.22, 0.18) if pieces else 1.0
    values = jax.random.normal(own_key, dims, jnp.float32) * width * loudness
    return jnp.minimum(jnp.maximum(values, -most), most).astype(kind)


def setup_inputs(seed: int = 0) -> dict:
    splits = jax.random.split(jax.random.key(seed), 6)
    tokens = gaussian(splits[0], (TOKENS, D), 1.0, 6.0, ((0, 32), (1, 8)))
    gate_weight = gaussian(splits[1], (D, SLAB), D ** -0.5, 0.046875, ((1, 8),))
    up_weight = gaussian(splits[2], (D, SLAB), D ** -0.5, 0.046875, ((1, 8),))
    hidden_grad = gaussian(splits[3], (TOKENS, SLAB), 1.0, 6.0, ((0, 32), (1, 8)))
    mb_lengths = draw_mb_lengths(jax.random.fold_in(splits[5], 71), 0)
    return dict(tokens=tokens, gate_weight=gate_weight, up_weight=up_weight, hidden_grad=hidden_grad, mb_lengths=mb_lengths)


def row_weights(lengths_table, capacity):
    mb_ends = jnp.cumsum(lengths_table, axis=1)
    mb_starts = mb_ends - lengths_table
    offsets = jnp.arange(capacity, dtype=jnp.int32)[None, :, None]
    inside_mb = (offsets >= mb_starts[:, None, :]) & (offsets < mb_ends[:, None, :])
    inverse = 1.0 / lengths_table.astype(jnp.float32)
    return jnp.sum(jnp.where(inside_mb, inverse[:, None, :], jnp.float32(0.0)), axis=2)


def reference(tokens, gate_weight, up_weight, hidden_grad, mb_lengths):
    gate_pre = jnp.dot(tokens, gate_weight, preferred_element_type=jnp.float32)
    up_pre = jnp.dot(tokens, up_weight, preferred_element_type=jnp.float32)
    row_scale = row_weights(mb_lengths, TOK_DEV).reshape(TOKENS)[:, None]
    sig_gate = jax.nn.sigmoid(gate_pre)
    scaled = row_scale * hidden_grad.astype(jnp.float32)
    grad_gate_pre = (scaled * up_pre * sig_gate * (1.0 + gate_pre * (1.0 - sig_gate))).astype(jnp.bfloat16)
    grad_up_pre = (scaled * gate_pre * sig_gate).astype(jnp.bfloat16)
    gate_grad = jnp.dot(tokens.T, grad_gate_pre, preferred_element_type=jnp.float32)
    up_grad = jnp.dot(tokens.T, grad_up_pre, preferred_element_type=jnp.float32)
    return gate_grad, up_grad
```

```python
import jax
import jax.numpy as jnp
from jax import lax
from jax.sharding import Mesh, PartitionSpec as P

NY, NZ, NX, NC = 4, 8, 4, 2
SIZES = {"y": NY, "z": NZ, "x": NX, "c": NC}
F32, BF16 = jnp.float32, jnp.bfloat16


def shift(value, axis, by):
    n = SIZES[axis]
    return lax.ppermute(value, axis, [(i, (i + by) % n) for i in range(n)])


def row_weights(lengths_table, capacity):
    mb_ends = jnp.cumsum(lengths_table, axis=1)
    mb_starts = mb_ends - lengths_table
    offsets = jnp.arange(capacity, dtype=jnp.int32)[None, :, None]
    inside_mb = (offsets >= mb_starts[:, None, :]) & (offsets < mb_ends[:, None, :])
    inverse = 1.0 / lengths_table.astype(F32)
    return jnp.sum(jnp.where(inside_mb, inverse[:, None, :], F32(0.0)), axis=2)


def ring_gather(block, axis):
    half = block.shape[0] // 2
    top, bottom = block[:half], block[half:]
    left_top = shift(top, axis, 1)
    right_bottom = shift(bottom, axis, -1)
    left_bottom = shift(bottom, axis, 1)
    right_top = shift(top, axis, -1)
    far_top = shift(left_top, axis, 1)
    far_bottom = shift(right_bottom, axis, -1)
    return [(top, bottom), (right_top, right_bottom), (far_top, far_bottom), (left_top, left_bottom)]


def dot(a, b):
    return jnp.dot(a, b, preferred_element_type=F32)


def dot_t(a, b):
    return lax.dot_general(a, b, (((0,), (0,)), ((), ())), preferred_element_type=F32)


def shards(tokens, gate_weight, up_weight, hidden_grad, mb_lengths):
    x, y, z, c = (lax.axis_index(a) for a in "xyzc")
    slots, feats = tokens.shape
    cols = gate_weight.shape[1]
    chunk = feats // 16

    ring = ring_gather(tokens, "x")

    def weight_rows(e, core):
        start = (((x + e) % NX) * NC + core) * feats
        return jnp.concatenate(
            [lax.dynamic_slice_in_dim(w, start, feats, 0) for w in (gate_weight, up_weight)], axis=1
        )

    own_w = [weight_rows(e, c) for e in range(NX)]
    other_w = [shift(weight_rows(e, 1 - c), "c", 1) for e in range(NX)]

    def feature_slice(d):
        place = ((y + d) % NY) * chunk
        return jnp.concatenate(
            [lax.dynamic_slice_in_dim(tokens, q * NY * chunk + place, chunk, 1) for q in range(4)], axis=1
        )

    plane = []
    for d in range(NY):
        piece = feature_slice((NY - d) % NY)
        if d:
            piece = shift(piece, "y", (NY - d) % NY)
        plane.append(jnp.concatenate([piece, shift(piece, "c", 1)], axis=1))

    def partial(weights):
        halves = []
        for h in range(2):
            total = None
            for e in range(NX):
                term = dot(ring[e][h], weights[e])
                total = term if total is None else total + term
            halves.append(total)
        return jnp.concatenate(halves, axis=0)

    pre = partial(own_w) + shift(partial(other_w), "c", 1)
    gate_pre, up_pre = pre[:, :cols], pre[:, cols:]
    row_scale = row_weights(mb_lengths, slots)[0][:, None]
    sig = jax.nn.sigmoid(gate_pre)
    scaled = row_scale * hidden_grad.astype(F32)
    grads = (
        (scaled * up_pre * sig * (1.0 + gate_pre * (1.0 - sig))).astype(BF16),
        (scaled * gate_pre * sig).astype(BF16),
    )

    outs = []
    for grad in grads:
        wide = jnp.concatenate(
            [grad, shift(grad, "x", -1), shift(grad, "x", 2), shift(grad, "x", 1)], axis=1
        )
        blocks = ring_gather(wide, "y")
        half = slots // 2
        total = None
        for d in range(NY):
            for h in range(2):
                term = dot_t(plane[d][h * half : (h + 1) * half], blocks[d][h])
                total = term if total is None else total + term

        def part(k):
            return lax.dynamic_slice_in_dim(total, ((z + k + 4 * c) % NZ) * chunk, chunk, 0)

        hc = chunk // 2
        low3 = shift(part(-3).astype(BF16), "z", -1)
        high3 = shift(part(3).astype(BF16), "z", 1)
        far = part(4).astype(BF16)
        low4 = shift(far[:hc], "z", -2)
        high4 = shift(far[hc:], "z", 2)
        zero = jnp.zeros((chunk - hc, total.shape[1]), F32)
        low2 = part(-2) + low3.astype(F32) + jnp.concatenate([low4.astype(F32), zero], axis=0)
        high2 = part(2) + high3.astype(F32) + jnp.concatenate([zero, high4.astype(F32)], axis=0)
        low2 = shift(low2.astype(BF16), "z", -2)
        high2 = shift(high2.astype(BF16), "z", 2)
        low1 = shift(part(-1).astype(BF16), "z", -1)
        high1 = shift(part(1).astype(BF16), "z", 1)
        mine = part(0) + low1.astype(F32) + high1.astype(F32) + low2.astype(F32) + high2.astype(F32)

        by_x = jnp.stack(
            [mine[:, :cols]] + [shift(mine[:, e * cols : (e + 1) * cols], "x", e) for e in range(1, NX)]
        )
        out = jnp.zeros((NY * chunk, cols), F32)
        for d in range(NY):
            piece = lax.dynamic_index_in_dim(by_x, (x - y - d) % NX, 0, keepdims=False)
            if d:
                piece = shift(piece, "y", d)
            out = lax.dynamic_update_slice_in_dim(out, piece, ((y - d) % NY) * chunk, 0)
        outs.append(out)
    return tuple(outs)


def solution(mesh):
    fine = Mesh(mesh.devices.reshape(NY, NZ, NX, NC), ("y", "z", "x", "c"))
    dp, tensor = ("y", "z"), ("x", "c")
    return jax.shard_map(
        shards,
        mesh=fine,
        in_specs=(P(dp, tensor), P(None, tensor), P(None, tensor), P(dp, tensor), P(dp, None)),
        out_specs=(P(dp, tensor), P(dp, tensor)),
        check_vma=False,
    )
```

```python
import jax
import jax.numpy as jnp
from jax import lax
from jax.experimental import pallas as pl
from jax.experimental.pallas import tpu as pltpu
from jax.sharding import Mesh, PartitionSpec as P

NY, NZ, NX, NC = 4, 8, 4, 2
SIZES = {"y": NY, "z": NZ, "x": NX, "c": NC}
F32, BF16 = jnp.float32, jnp.bfloat16


def shift(value, axis, by):
    n = SIZES[axis]
    return lax.ppermute(value, axis, [(i, (i + by) % n) for i in range(n)])


def row_weights(lengths_table, capacity):
    mb_ends = jnp.cumsum(lengths_table, axis=1)
    mb_starts = mb_ends - lengths_table
    offsets = jnp.arange(capacity, dtype=jnp.int32)[None, :, None]
    inside_mb = (offsets >= mb_starts[:, None, :]) & (offsets < mb_ends[:, None, :])
    inverse = 1.0 / lengths_table.astype(F32)
    return jnp.sum(jnp.where(inside_mb, inverse[:, None, :], F32(0.0)), axis=2)


def ring_gather(block, axis):
    half = block.shape[0] // 2
    left = shift(block, axis, 1)
    right = shift(block, axis, -1)
    far = (shift(left[:half], axis, 1), shift(right[half:], axis, -1))
    return [(block,), (right,), far, (left,)]


def after(value, *earlier):
    return lax.optimization_barrier((value, *earlier))[0]


def dot(a, b):
    return jnp.dot(a, b, preferred_element_type=F32)


def row_tiles(total, tile, body):
    @pl.loop(0, total // tile)
    def _(i):
        body(pl.ds(pl.multiple_of(i * tile, tile), tile))


def gate_kernel(at_y, left, own, right, before, out):
    def body(rows):
        out[rows, :] = sum(
            dot(left[at_y[d], rows, :], block[...]) for d, block in zip((0, 1, 3), (own, right, before))
        )

    row_tiles(out.shape[0], out.shape[0] // 4, body)


def up_kernel(at_y, left, own, right, before, out, side):
    cols = own.shape[1]
    depth = left.shape[2]
    for i, block in enumerate((own, right, before)):
        side[:, i * cols : (i + 1) * cols] = block[...]

    def body(rows):
        out[rows, :] = sum(
            dot(left[at_y[d], rows, :], side[d * depth : (d + 1) * depth, :]) for d in range(NY)
        )

    row_tiles(out.shape[0], out.shape[0] // 4, body)


def last_kernel(at_y, order, left, gate, up, far_top, far_bottom, far_up, *refs):
    low3, high3, low1, high1, far_low, far_high, kept, far_gate = refs
    half, cols, depth = far_top.shape[0], far_up.shape[1], left.shape[2]
    chunk, wide = kept.shape[1], gate.shape[1]
    far_gate[:half, :] = far_top[...]
    far_gate[half:, :] = far_bottom[...]

    def part(k, outs):
        rows = pl.ds(pl.multiple_of(order[k % NZ] * chunk, chunk), chunk)
        tiles = [left[at_y[d], rows, :] for d in range(NY)]
        ups = up[rows, :]
        parts = (
            (0, gate[rows, :] + dot(tiles[2], far_gate[...])),
            (wide, ups[:, : 2 * cols]),
            (
                wide + 2 * cols,
                sum(dot(tiles[d], far_up[d * depth : (d + 1) * depth, :]) for d in range(NY)),
            ),
            (wide + 3 * cols, ups[:, 2 * cols :]),
        )
        for start, value in parts:
            place = pl.ds(start, value.shape[1])
            for out, at, size in outs:
                piece = value[at : at + size, :].astype(out.dtype)
                out[:, place] = piece

    part(-3, [(low3, 0, chunk)])
    part(3, [(high3, 0, chunk)])
    part(4, [(far_low, 0, chunk // 2), (far_high, chunk // 2, chunk // 2)])
    part(-1, [(low1, 0, chunk)])
    part(1, [(high1, 0, chunk)])
    for i, k in enumerate((0, -2, 2)):
        part(k, [(kept.at[i], 0, chunk)])


VMEM = pl.BlockSpec(memory_space=pltpu.VMEM)
SMEM = pl.BlockSpec(memory_space=pltpu.SMEM)
PARAMS = pltpu.CompilerParams(vmem_limit_bytes=13 * 1024 * 1024)


def cost(flops, size):
    return pl.CostEstimate(flops=flops, bytes_accessed=size, transcendentals=0)


def gate_products(at_y, left, blocks):
    _, rows, depth = left.shape
    wide = blocks[0].shape[1]
    return pl.pallas_call(
        gate_kernel,
        out_shape=jax.ShapeDtypeStruct((rows, wide), F32),
        in_specs=[SMEM] + [VMEM] * 4,
        out_specs=VMEM,
        compiler_params=PARAMS,
        cost_estimate=cost(6 * rows * depth * wide, 4 * rows * wide),
        name="gate_products",
    )(at_y, left, *blocks)


def up_products(at_y, left, blocks):
    _, rows, depth = left.shape
    wide = 3 * blocks[0].shape[1]
    return pl.pallas_call(
        up_kernel,
        out_shape=jax.ShapeDtypeStruct((rows, wide), F32),
        in_specs=[SMEM] + [VMEM] * 4,
        out_specs=VMEM,
        scratch_shapes=[pltpu.VMEM((NY * depth, wide), BF16)],
        compiler_params=PARAMS,
        cost_estimate=cost(8 * rows * depth * wide, 4 * rows * wide),
        name="up_products",
    )(at_y, left, *blocks)


def last_products(at_y, order, left, gate, up, far_top, far_bottom, far_up):
    _, rows, depth = left.shape
    cols = far_up.shape[1]
    chunk = rows // NZ
    near = jax.ShapeDtypeStruct((chunk, 8 * cols), BF16)
    far = jax.ShapeDtypeStruct((chunk // 2, 8 * cols), BF16)
    kept = jax.ShapeDtypeStruct((3, chunk, 8 * cols), F32)
    return pl.pallas_call(
        last_kernel,
        out_shape=(near, near, near, near, far, far, kept),
        in_specs=[SMEM] * 2 + [VMEM] * 6,
        out_specs=(VMEM,) * 7,
        scratch_shapes=[pltpu.VMEM((depth, 4 * cols), BF16)],
        compiler_params=PARAMS,
        cost_estimate=cost(16 * rows * depth * cols, 8 * rows * 8 * cols),
        name="last_products",
    )(at_y, order, left, gate, up, far_top, far_bottom, far_up)


def shards(tokens, gate_weight, up_weight, hidden_grad, mb_lengths):
    x, y, z, c = (lax.axis_index(a) for a in "xyzc")
    slots, feats = tokens.shape
    cols = gate_weight.shape[1]
    chunk = feats // 16

    half = slots // 2
    top, bottom = tokens[:half], tokens[half:]
    left_top, right_bottom = shift(top, "x", 1), shift(bottom, "x", -1)
    left_bottom, right_top = shift(bottom, "x", 1), shift(top, "x", -1)
    far_top, far_bottom = shift(left_top, "x", 1), shift(right_bottom, "x", -1)
    ring = [(top, bottom), (right_top, right_bottom), (far_top, far_bottom), (left_top, left_bottom)]

    pieces = jnp.stack(
        [
            jnp.concatenate(
                [tokens[:, (q * NY + j) * chunk : (q * NY + j + 1) * chunk] for q in range(4)], axis=1
            )
            for j in range(NY)
        ]
    )
    pieces = lax.all_to_all(pieces, "y", 0, 0, tiled=True)
    plane = jnp.concatenate(
        [v.transpose(0, 2, 1) for v in (pieces, shift(pieces, "c", 1))], axis=1
    )

    weights = [after(w, pieces) for w in (gate_weight, up_weight)]

    def weight_rows(e, core):
        start = (((x + e) % NX) * NC + core) * feats
        return jnp.concatenate([lax.dynamic_slice_in_dim(w, start, feats, 0) for w in weights], axis=1)

    own_w = [weight_rows(e, c) for e in range(NX)]
    other_w = [shift(weight_rows(e, 1 - c), "c", 1) for e in range(NX)]

    def near(w):
        return [sum(dot(ring[e][h], w[e]) for e in (0, 1, 3)) for h in range(2)]

    own, other = near(own_w), near(other_w)
    far_rows = [after(r, *own, *other, plane) for r in ring[2]]
    other = jnp.concatenate([o + dot(r, other_w[2]) for o, r in zip(other, far_rows)], axis=0)
    own = jnp.concatenate([o + dot(r, own_w[2]) for o, r in zip(own, far_rows)], axis=0)
    pre = own + shift(other, "c", 1)
    gate_pre, up_pre = pre[:, :cols], pre[:, cols:]

    row_scale = row_weights(mb_lengths, slots)[0][:, None]
    sig = jax.nn.sigmoid(gate_pre)
    scaled = row_scale * hidden_grad.astype(F32)
    grad_gate = (scaled * up_pre * sig * (1.0 + gate_pre * (1.0 - sig))).astype(BF16)
    grad_up = (scaled * gate_pre * sig).astype(BF16)

    def around(value, axis):
        return [value, shift(value, axis, -1), shift(value, axis, 2), shift(value, axis, 1)]

    wide_gate = jnp.concatenate(around(grad_gate, "x"), axis=1)
    tall_up = jnp.concatenate(around(grad_up, "y"), axis=0)
    gates = ring_gather(wide_gate, "y")
    ups = around(tall_up, "x")

    at_y = jnp.stack([(y + d) % NY for d in range(NY)]).astype(jnp.int32)
    order = jnp.stack([(z + k + 4 * c) % NZ for k in range(NZ)]).astype(jnp.int32)
    near = (0, 1, 3)
    gate_sum = gate_products(at_y, plane, [gates[d][0] for d in near])
    up_sum = up_products(at_y, plane, [ups[e] for e in near])
    low3, high3, low1, high1, far_low, far_high, kept = last_products(
        at_y, order, plane, gate_sum, up_sum, *gates[2], ups[2]
    )

    low3, high3 = shift(low3, "z", -1), shift(high3, "z", 1)
    far_low, far_high = shift(far_low, "z", -2), shift(far_high, "z", 2)
    low1, high1 = shift(low1, "z", -1), shift(high1, "z", 1)
    zero = jnp.zeros((chunk - chunk // 2, far_low.shape[1]), F32)
    low2 = kept[1] + low3.astype(F32) + jnp.concatenate([far_low.astype(F32), zero], axis=0)
    high2 = kept[2] + high3.astype(F32) + jnp.concatenate([zero, far_high.astype(F32)], axis=0)
    low2, high2 = shift(low2.astype(BF16), "z", -2), shift(high2.astype(BF16), "z", 2)
    mine = kept[0] + low1.astype(F32) + high1.astype(F32) + low2.astype(F32) + high2.astype(F32)
    mine = [mine[:, : NX * cols], mine[:, NX * cols :]]

    both = jnp.stack(mine)
    outs = [jnp.zeros((NY * chunk, cols), F32)] * 2
    for m in range(NX):
        piece = lax.dynamic_slice_in_dim(both, ((y + m - x) % NX) * cols, cols, 2)
        pairs = [(j * NX + i, i * NX + (j + m) % NX) for j in range(NY) for i in range(NX)]
        piece = lax.ppermute(piece, ("y", "x"), pairs)
        place = ((x - m) % NX) * chunk
        outs = [lax.dynamic_update_slice_in_dim(o, p, place, 0) for o, p in zip(outs, piece)]
    return tuple(outs)


def solution(mesh):
    fine = Mesh(mesh.devices.reshape(NY, NZ, NX, NC), ("y", "z", "x", "c"))
    dp, tensor = ("y", "z"), ("x", "c")
    return jax.shard_map(
        shards,
        mesh=fine,
        in_specs=(P(dp, tensor), P(None, tensor), P(None, tensor), P(dp, tensor), P(dp, None)),
        out_specs=(P(dp, tensor), P(dp, tensor)),
        check_vma=False,
    )
```

```python
import jax
import jax.numpy as jnp
from jax import lax
from jax.experimental import pallas as pl
from jax.experimental.pallas import tpu as pltpu
from jax.sharding import Mesh, PartitionSpec as P

NY, NZ, NX, NC = 4, 8, 4, 2
SIZES = {"y": NY, "z": NZ, "x": NX, "c": NC}
F32, BF16 = jnp.float32, jnp.bfloat16


def shift(value, axis, by):
    n = SIZES[axis]
    return lax.ppermute(value, axis, [(i, (i + by) % n) for i in range(n)])


def row_weights(lengths_table, capacity):
    mb_ends = jnp.cumsum(lengths_table, axis=1)
    mb_starts = mb_ends - lengths_table
    offsets = jnp.arange(capacity, dtype=jnp.int32)[None, :, None]
    inside_mb = (offsets >= mb_starts[:, None, :]) & (offsets < mb_ends[:, None, :])
    inverse = 1.0 / lengths_table.astype(F32)
    return jnp.sum(jnp.where(inside_mb, inverse[:, None, :], F32(0.0)), axis=2)


def ring_gather(block, axis):
    half = block.shape[0] // 2
    left = shift(block, axis, 1)
    right = shift(block, axis, -1)
    far = (shift(left[:half], axis, 1), shift(right[half:], axis, -1))
    return [(block,), (right,), far, (left,)]


def after(value, *earlier):
    return lax.optimization_barrier((value, *earlier))[0]


def dot(a, b):
    return jnp.dot(a, b, preferred_element_type=F32)


def row_tiles(total, tile, body):
    @pl.loop(0, total // tile)
    def _(i):
        body(pl.ds(pl.multiple_of(i * tile, tile), tile))


def gate_kernel(at_y, left, own, right, before, out):
    def body(rows):
        out[rows, :] = sum(
            dot(left[at_y[d], rows, :], block[...]) for d, block in zip((0, 1, 3), (own, right, before))
        )

    row_tiles(out.shape[0], out.shape[0] // 4, body)


def up_kernel(at_y, left, own, right, before, out, side):
    cols = own.shape[1]
    depth = left.shape[2]
    for i, block in enumerate((own, right, before)):
        side[:, i * cols : (i + 1) * cols] = block[...]

    def body(rows):
        out[rows, :] = sum(
            dot(left[at_y[d], rows, :], side[d * depth : (d + 1) * depth, :]) for d in range(NY)
        )

    row_tiles(out.shape[0], out.shape[0] // 4, body)


def last_kernel(at_y, order, left, gate, up, far_top, far_bottom, far_up, *refs):
    low3, high3, low1, high1, far_low, far_high, kept, far_gate = refs
    half, cols, depth = far_top.shape[0], far_up.shape[1], left.shape[2]
    chunk, wide = kept.shape[1], gate.shape[1]
    far_gate[:half, :] = far_top[...]
    far_gate[half:, :] = far_bottom[...]

    def part(k, outs):
        rows = pl.ds(pl.multiple_of(order[k % NZ] * chunk, chunk), chunk)
        tiles = [left[at_y[d], rows, :] for d in range(NY)]
        ups = up[rows, :]
        parts = (
            (0, gate[rows, :] + dot(tiles[2], far_gate[...])),
            (wide, ups[:, : 2 * cols]),
            (
                wide + 2 * cols,
                sum(dot(tiles[d], far_up[d * depth : (d + 1) * depth, :]) for d in range(NY)),
            ),
            (wide + 3 * cols, ups[:, 2 * cols :]),
        )
        for start, value in parts:
            place = pl.ds(start, value.shape[1])
            for out, at, size in outs:
                piece = value[at : at + size, :].astype(out.dtype)
                out[:, place] = piece

    part(-3, [(low3, 0, chunk)])
    part(3, [(high3, 0, chunk)])
    part(4, [(far_low, 0, chunk // 2), (far_high, chunk // 2, chunk // 2)])
    part(-1, [(low1, 0, chunk)])
    part(1, [(high1, 0, chunk)])
    for i, k in enumerate((0, -2, 2)):
        part(k, [(kept.at[i], 0, chunk)])


VMEM = pl.BlockSpec(memory_space=pltpu.VMEM)
SMEM = pl.BlockSpec(memory_space=pltpu.SMEM)
PARAMS = pltpu.CompilerParams(vmem_limit_bytes=13 * 1024 * 1024)


def cost(flops, size):
    return pl.CostEstimate(flops=flops, bytes_accessed=size, transcendentals=0)


def far_kernel(top, bottom, own_w, other_w, own_top, own_bottom, other_top, other_bottom, own, other):
    half = top.shape[0]
    for out, w, sums in ((other, other_w, (other_top, other_bottom)), (own, own_w, (own_top, own_bottom))):
        for i, rows in enumerate((top, bottom)):
            out[i * half : (i + 1) * half, :] = sums[i][...] + dot(rows[...], w[...])


def far_products(rows, own_w, other_w, own, other):
    half, depth = rows[0].shape
    cols = own_w.shape[1]
    out = jax.ShapeDtypeStruct((2 * half, cols), F32)
    return pl.pallas_call(
        far_kernel,
        out_shape=(out, out),
        in_specs=[VMEM] * 8,
        out_specs=(VMEM, VMEM),
        compiler_params=PARAMS,
        cost_estimate=cost(8 * half * depth * cols, 8 * half * depth),
        name="far_products",
    )(*rows, own_w, other_w, *own, *other)


def gate_products(at_y, left, blocks):
    _, rows, depth = left.shape
    wide = blocks[0].shape[1]
    return pl.pallas_call(
        gate_kernel,
        out_shape=jax.ShapeDtypeStruct((rows, wide), F32),
        in_specs=[SMEM] + [VMEM] * 4,
        out_specs=VMEM,
        compiler_params=PARAMS,
        cost_estimate=cost(6 * rows * depth * wide, 4 * rows * wide),
        name="gate_products",
    )(at_y, left, *blocks)


def up_products(at_y, left, blocks):
    _, rows, depth = left.shape
    wide = 3 * blocks[0].shape[1]
    return pl.pallas_call(
        up_kernel,
        out_shape=jax.ShapeDtypeStruct((rows, wide), F32),
        in_specs=[SMEM] + [VMEM] * 4,
        out_specs=VMEM,
        scratch_shapes=[pltpu.VMEM((NY * depth, wide), BF16)],
        compiler_params=PARAMS,
        cost_estimate=cost(8 * rows * depth * wide, 4 * rows * wide),
        name="up_products",
    )(at_y, left, *blocks)


def last_products(at_y, order, left, gate, up, far_top, far_bottom, far_up):
    _, rows, depth = left.shape
    cols = far_up.shape[1]
    chunk = rows // NZ
    near = jax.ShapeDtypeStruct((chunk, 8 * cols), BF16)
    far = jax.ShapeDtypeStruct((chunk // 2, 8 * cols), BF16)
    kept = jax.ShapeDtypeStruct((3, chunk, 8 * cols), F32)
    return pl.pallas_call(
        last_kernel,
        out_shape=(near, near, near, near, far, far, kept),
        in_specs=[SMEM] * 2 + [VMEM] * 6,
        out_specs=(VMEM,) * 7,
        scratch_shapes=[pltpu.VMEM((depth, 4 * cols), BF16)],
        compiler_params=PARAMS,
        cost_estimate=cost(16 * rows * depth * cols, 8 * rows * 8 * cols),
        name="last_products",
    )(at_y, order, left, gate, up, far_top, far_bottom, far_up)


def shards(tokens, gate_weight, up_weight, hidden_grad, mb_lengths):
    x, y, z, c = (lax.axis_index(a) for a in "xyzc")
    slots, feats = tokens.shape
    cols = gate_weight.shape[1]
    chunk = feats // 16

    half = slots // 2
    top, bottom = tokens[:half], tokens[half:]
    left_top, right_bottom = shift(top, "x", 1), shift(bottom, "x", -1)
    left_bottom, right_top = shift(bottom, "x", 1), shift(top, "x", -1)
    far_top, far_bottom = shift(left_top, "x", 1), shift(right_bottom, "x", -1)
    ring = [(top, bottom), (right_top, right_bottom), (far_top, far_bottom), (left_top, left_bottom)]

    pieces = jnp.stack(
        [
            jnp.concatenate(
                [tokens[:, (q * NY + j) * chunk : (q * NY + j + 1) * chunk] for q in range(4)], axis=1
            )
            for j in range(NY)
        ]
    )
    pieces = lax.optimization_barrier(lax.all_to_all(pieces, "y", 0, 0, tiled=True))
    plane = jnp.concatenate(
        [v.transpose(0, 2, 1) for v in (pieces, shift(pieces, "c", 1))], axis=1
    )

    weights = [after(w, pieces) for w in (gate_weight, up_weight)]

    def weight_rows(e, core):
        start = (((x + e) % NX) * NC + core) * feats
        return jnp.concatenate([lax.dynamic_slice_in_dim(w, start, feats, 0) for w in weights], axis=1)

    own_w = [weight_rows(e, c) for e in range(NX)]
    other_w = [shift(weight_rows(e, 1 - c), "c", 1) for e in range(NX)]

    def near(w):
        return [sum(dot(ring[e][h], w[e]) for e in (0, 1, 3)) for h in range(2)]

    own, other = near(own_w), near(other_w)
    far_rows = [after(r, *own, *other, plane) for r in ring[2]]
    own, other = far_products(far_rows, own_w[2], other_w[2], own, other)
    pre = own + shift(other, "c", 1)
    gate_pre, up_pre = pre[:, :cols], pre[:, cols:]

    row_scale = row_weights(mb_lengths, slots)[0][:, None]
    sig = jax.nn.sigmoid(gate_pre)
    scaled = row_scale * hidden_grad.astype(F32)
    grad_gate = (scaled * up_pre * sig * (1.0 + gate_pre * (1.0 - sig))).astype(BF16)
    grad_up = (scaled * gate_pre * sig).astype(BF16)

    def around(value, axis):
        return [value, shift(value, axis, -1), shift(value, axis, 2), shift(value, axis, 1)]

    wide_gate = jnp.concatenate(around(grad_gate, "x"), axis=1)
    tall_up = jnp.concatenate(around(grad_up, "y"), axis=0)
    gates = ring_gather(wide_gate, "y")
    ups = around(tall_up, "x")

    at_y = jnp.stack([(y + d) % NY for d in range(NY)]).astype(jnp.int32)
    order = jnp.stack([(z + k + 4 * c) % NZ for k in range(NZ)]).astype(jnp.int32)
    near = (0, 1, 3)
    gate_sum = gate_products(at_y, plane, [gates[d][0] for d in near])
    up_sum = up_products(at_y, plane, [ups[e] for e in near])
    low3, high3, low1, high1, far_low, far_high, kept = last_products(
        at_y, order, plane, gate_sum, up_sum, *gates[2], ups[2]
    )

    low3, high3 = shift(low3, "z", -1), shift(high3, "z", 1)
    far_low, far_high = shift(far_low, "z", -2), shift(far_high, "z", 2)
    low1, high1 = shift(low1, "z", -1), shift(high1, "z", 1)
    zero = jnp.zeros((chunk - chunk // 2, far_low.shape[1]), F32)
    low2 = kept[1] + low3.astype(F32) + jnp.concatenate([far_low.astype(F32), zero], axis=0)
    high2 = kept[2] + high3.astype(F32) + jnp.concatenate([zero, far_high.astype(F32)], axis=0)
    low2, high2 = shift(low2.astype(BF16), "z", -2), shift(high2.astype(BF16), "z", 2)
    mine = kept[0] + low1.astype(F32) + high1.astype(F32) + low2.astype(F32) + high2.astype(F32)
    mine = [mine[:, : NX * cols], mine[:, NX * cols :]]

    both = jnp.stack(mine)
    outs = [jnp.zeros((NY * chunk, cols), F32)] * 2
    for m in range(NX):
        piece = lax.dynamic_slice_in_dim(both, ((y + m - x) % NX) * cols, cols, 2)
        pairs = [(j * NX + i, i * NX + (j + m) % NX) for j in range(NY) for i in range(NX)]
        piece = lax.ppermute(piece, ("y", "x"), pairs)
        place = ((x - m) % NX) * chunk
        outs = [lax.dynamic_update_slice_in_dim(o, p, place, 0) for o, p in zip(outs, piece)]
    return tuple(outs)


def solution(mesh):
    fine = Mesh(mesh.devices.reshape(NY, NZ, NX, NC), ("y", "z", "x", "c"))
    dp, tensor = ("y", "z"), ("x", "c")
    return jax.shard_map(
        shards,
        mesh=fine,
        in_specs=(P(dp, tensor), P(None, tensor), P(None, tensor), P(dp, tensor), P(dp, None)),
        out_specs=(P(dp, tensor), P(dp, tensor)),
        check_vma=False,
    )
```

```python
import jax
import jax.numpy as jnp
from jax import lax
from jax.experimental import pallas as pl
from jax.experimental.pallas import tpu as pltpu
from jax.sharding import Mesh, PartitionSpec as P

NY, NZ, NX, NC = 4, 8, 4, 2
SIZES = {"y": NY, "z": NZ, "x": NX, "c": NC}
F32, BF16 = jnp.float32, jnp.bfloat16


def shift(value, axis, by):
    n = SIZES[axis]
    return lax.ppermute(value, axis, [(i, (i + by) % n) for i in range(n)])


def row_weights(lengths_table, capacity):
    mb_ends = jnp.cumsum(lengths_table, axis=1)
    mb_starts = mb_ends - lengths_table
    offsets = jnp.arange(capacity, dtype=jnp.int32)[None, :, None]
    inside_mb = (offsets >= mb_starts[:, None, :]) & (offsets < mb_ends[:, None, :])
    inverse = 1.0 / lengths_table.astype(F32)
    return jnp.sum(jnp.where(inside_mb, inverse[:, None, :], F32(0.0)), axis=2)


def ring_gather(block, axis):
    half = block.shape[0] // 2
    left = shift(block, axis, 1)
    right = shift(block, axis, -1)
    far = (shift(left[:half], axis, 1), shift(right[half:], axis, -1))
    return [(block,), (right,), far, (left,)]


def after(value, *earlier):
    return lax.optimization_barrier((value, *earlier))[0]


def dot(a, b):
    return jnp.dot(a, b, preferred_element_type=F32)


def row_tiles(total, tile, body):
    @pl.loop(0, total // tile)
    def _(i):
        body(pl.ds(pl.multiple_of(i * tile, tile), tile))


def gate_kernel(at_y, left, own, right, before, out):
    def body(rows):
        out[rows, :] = sum(
            dot(left[at_y[d], rows, :], block[...]) for d, block in zip((0, 1, 3), (own, right, before))
        )

    row_tiles(out.shape[0], out.shape[0] // 4, body)


def up_kernel(at_y, left, own, right, before, out, side):
    cols = own.shape[1]
    depth = left.shape[2]
    for i, block in enumerate((own, right, before)):
        side[:, i * cols : (i + 1) * cols] = block[...]

    def body(rows):
        out[rows, :] = sum(
            dot(left[at_y[d], rows, :], side[d * depth : (d + 1) * depth, :]) for d in range(NY)
        )

    row_tiles(out.shape[0], out.shape[0] // 4, body)


def last_kernel(at_y, order, left, gate, up, far_top, far_bottom, far_up, *refs):
    low3, high3, low1, high1, far_low, far_high, kept, far_gate = refs
    half, cols, depth = far_top.shape[0], far_up.shape[1], left.shape[2]
    chunk, wide = kept.shape[1], gate.shape[1]
    far_gate[:half, :] = far_top[...]
    far_gate[half:, :] = far_bottom[...]

    def part(k, outs):
        rows = pl.ds(pl.multiple_of(order[k % NZ] * chunk, chunk), chunk)
        tiles = [left[at_y[d], rows, :] for d in range(NY)]
        ups = up[rows, :]
        parts = (
            (0, gate[rows, :] + dot(tiles[2], far_gate[...])),
            (wide, ups[:, : 2 * cols]),
            (
                wide + 2 * cols,
                sum(dot(tiles[d], far_up[d * depth : (d + 1) * depth, :]) for d in range(NY)),
            ),
            (wide + 3 * cols, ups[:, 2 * cols :]),
        )
        for start, value in parts:
            place = pl.ds(start, value.shape[1])
            for out, at, size in outs:
                piece = value[at : at + size, :].astype(out.dtype)
                out[:, place] = piece

    part(-3, [(low3, 0, chunk)])
    part(3, [(high3, 0, chunk)])
    part(4, [(far_low, 0, chunk // 2), (far_high, chunk // 2, chunk // 2)])
    part(-1, [(low1, 0, chunk)])
    part(1, [(high1, 0, chunk)])
    for i, k in enumerate((0, -2, 2)):
        part(k, [(kept.at[i], 0, chunk)])


VMEM = pl.BlockSpec(memory_space=pltpu.VMEM)
SMEM = pl.BlockSpec(memory_space=pltpu.SMEM)
PARAMS = pltpu.CompilerParams(vmem_limit_bytes=13 * 1024 * 1024)


def cost(flops, size):
    return pl.CostEstimate(flops=flops, bytes_accessed=size, transcendentals=0)


def far_kernel(top, bottom, own_w, other_w, own_top, own_bottom, other_top, other_bottom, own, other):
    half = top.shape[0]
    for out, w, sums in ((other, other_w, (other_top, other_bottom)), (own, own_w, (own_top, own_bottom))):
        for i, rows in enumerate((top, bottom)):
            out[i * half : (i + 1) * half, :] = sums[i][...] + dot(rows[...], w[...])


def far_products(rows, own_w, other_w, own, other):
    half, depth = rows[0].shape
    cols = own_w.shape[1]
    out = jax.ShapeDtypeStruct((2 * half, cols), F32)
    return pl.pallas_call(
        far_kernel,
        out_shape=(out, out),
        in_specs=[VMEM] * 8,
        out_specs=(VMEM, VMEM),
        compiler_params=PARAMS,
        cost_estimate=cost(8 * half * depth * cols, 8 * half * depth),
        name="far_products",
    )(*rows, own_w, other_w, *own, *other)


def gate_products(at_y, left, blocks):
    _, rows, depth = left.shape
    wide = blocks[0].shape[1]
    return pl.pallas_call(
        gate_kernel,
        out_shape=jax.ShapeDtypeStruct((rows, wide), F32),
        in_specs=[SMEM] + [VMEM] * 4,
        out_specs=VMEM,
        compiler_params=PARAMS,
        cost_estimate=cost(6 * rows * depth * wide, 4 * rows * wide),
        name="gate_products",
    )(at_y, left, *blocks)


def up_products(at_y, left, blocks):
    _, rows, depth = left.shape
    wide = 3 * blocks[0].shape[1]
    return pl.pallas_call(
        up_kernel,
        out_shape=jax.ShapeDtypeStruct((rows, wide), F32),
        in_specs=[SMEM] + [VMEM] * 4,
        out_specs=VMEM,
        scratch_shapes=[pltpu.VMEM((NY * depth, wide), BF16)],
        compiler_params=PARAMS,
        cost_estimate=cost(8 * rows * depth * wide, 4 * rows * wide),
        name="up_products",
    )(at_y, left, *blocks)


def last_products(at_y, order, left, gate, up, far_top, far_bottom, far_up):
    _, rows, depth = left.shape
    cols = far_up.shape[1]
    chunk = rows // NZ
    near = jax.ShapeDtypeStruct((chunk, 8 * cols), BF16)
    far = jax.ShapeDtypeStruct((chunk // 2, 8 * cols), BF16)
    kept = jax.ShapeDtypeStruct((3, chunk, 8 * cols), F32)
    return pl.pallas_call(
        last_kernel,
        out_shape=(near, near, near, near, far, far, kept),
        in_specs=[SMEM] * 2 + [VMEM] * 6,
        out_specs=(VMEM,) * 7,
        scratch_shapes=[pltpu.VMEM((depth, 4 * cols), BF16)],
        compiler_params=PARAMS,
        cost_estimate=cost(16 * rows * depth * cols, 8 * rows * 8 * cols),
        name="last_products",
    )(at_y, order, left, gate, up, far_top, far_bottom, far_up)


def shards(tokens, gate_weight, up_weight, hidden_grad, mb_lengths):
    x, y, z, c = (lax.axis_index(a) for a in "xyzc")
    slots, feats = tokens.shape
    cols = gate_weight.shape[1]
    chunk = feats // 16

    half = slots // 2
    top, bottom = tokens[:half], tokens[half:]
    left_top, right_bottom = shift(top, "x", 1), shift(bottom, "x", -1)
    left_bottom, right_top = shift(bottom, "x", 1), shift(top, "x", -1)
    far_top, far_bottom = shift(left_top, "x", 1), shift(right_bottom, "x", -1)
    ring = [(top, bottom), (right_top, right_bottom), (far_top, far_bottom), (left_top, left_bottom)]

    pieces = tokens.T.reshape(4, NY, chunk, slots).transpose(1, 0, 2, 3).reshape(NY, 4 * chunk, slots)
    pieces = lax.all_to_all(pieces, "y", 0, 0, tiled=True)
    plane = jnp.concatenate([pieces, shift(pieces, "c", 1)], axis=1)

    weights = [after(w, pieces) for w in (gate_weight, up_weight)]

    def weight_rows(e, core):
        start = (((x + e) % NX) * NC + core) * feats
        return jnp.concatenate([lax.dynamic_slice_in_dim(w, start, feats, 0) for w in weights], axis=1)

    own_w = [weight_rows(e, c) for e in range(NX)]
    other_w = [shift(weight_rows(e, 1 - c), "c", 1) for e in range(NX)]

    def near(w):
        return [sum(dot(ring[e][h], w[e]) for e in (0, 1, 3)) for h in range(2)]

    own, other = near(own_w), near(other_w)
    far_rows = [after(r, *own, *other, plane) for r in ring[2]]
    own, other = far_products(far_rows, own_w[2], other_w[2], own, other)
    pre = own + shift(other, "c", 1)
    gate_pre, up_pre = pre[:, :cols], pre[:, cols:]

    row_scale = row_weights(mb_lengths, slots)[0][:, None]
    sig = jax.nn.sigmoid(gate_pre)
    scaled = row_scale * hidden_grad.astype(F32)
    grad_gate = (scaled * up_pre * sig * (1.0 + gate_pre * (1.0 - sig))).astype(BF16)
    grad_up = (scaled * gate_pre * sig).astype(BF16)

    def around(value, axis):
        return [value, shift(value, axis, -1), shift(value, axis, 2), shift(value, axis, 1)]

    wide_gate = jnp.concatenate(around(grad_gate, "x"), axis=1)
    tall_up = jnp.concatenate(around(grad_up, "y"), axis=0)
    gates = ring_gather(wide_gate, "y")
    ups = around(tall_up, "x")

    at_y = jnp.stack([(y + d) % NY for d in range(NY)]).astype(jnp.int32)
    order = jnp.stack([(z + k + 4 * c) % NZ for k in range(NZ)]).astype(jnp.int32)
    near = (0, 1, 3)
    gate_sum = gate_products(at_y, plane, [gates[d][0] for d in near])
    up_sum = up_products(at_y, plane, [ups[e] for e in near])
    low3, high3, low1, high1, far_low, far_high, kept = last_products(
        at_y, order, plane, gate_sum, up_sum, *gates[2], ups[2]
    )

    low3, high3 = shift(low3, "z", -1), shift(high3, "z", 1)
    far_low, far_high = shift(far_low, "z", -2), shift(far_high, "z", 2)
    low1, high1 = shift(low1, "z", -1), shift(high1, "z", 1)
    zero = jnp.zeros((chunk - chunk // 2, far_low.shape[1]), F32)
    low2 = kept[1] + low3.astype(F32) + jnp.concatenate([far_low.astype(F32), zero], axis=0)
    high2 = kept[2] + high3.astype(F32) + jnp.concatenate([zero, far_high.astype(F32)], axis=0)
    low2, high2 = shift(low2.astype(BF16), "z", -2), shift(high2.astype(BF16), "z", 2)
    mine = kept[0] + low1.astype(F32) + high1.astype(F32) + low2.astype(F32) + high2.astype(F32)
    mine = [mine[:, : NX * cols], mine[:, NX * cols :]]

    both = jnp.stack(mine)
    outs = [jnp.zeros((NY * chunk, cols), F32)] * 2
    for m in range(NX):
        piece = lax.dynamic_slice_in_dim(both, ((y + m - x) % NX) * cols, cols, 2)
        pairs = [(j * NX + i, i * NX + (j + m) % NX) for j in range(NY) for i in range(NX)]
        piece = lax.ppermute(piece, ("y", "x"), pairs)
        place = ((x - m) % NX) * chunk
        outs = [lax.dynamic_update_slice_in_dim(o, p, place, 0) for o, p in zip(outs, piece)]
    return tuple(outs)


def solution(mesh):
    fine = Mesh(mesh.devices.reshape(NY, NZ, NX, NC), ("y", "z", "x", "c"))
    dp, tensor = ("y", "z"), ("x", "c")
    return jax.shard_map(
        shards,
        mesh=fine,
        in_specs=(P(dp, tensor), P(None, tensor), P(None, tensor), P(dp, tensor), P(dp, None)),
        out_specs=(P(dp, tensor), P(dp, tensor)),
        check_vma=False,
    )
```
